256 devices in a mesh: row: 8 (over y, core), col: 4 (over x), depth: 8 (over z).
Axes of the slice: x: 4, y: 4, z: 8, core: 2. Of those that a mesh axis runs over, the one named last changes fastest.
Arguments:
- tokens: bfloat16 [2048, 6144], P(('depth', 'row'), 'col'), may hold values from -6 to 6
- weight: bfloat16 [6144, 24576], P('col', 'row'), may hold values from -0.078125 to 0.078125
- bias_term: float32 [24576], P('row'), may hold values from -1 to 1
- cotangent: bfloat16 [2048, 24576], P(('depth', 'col'), 'row'), may hold values from -100 to 100
Outputs:
- input_grad: bfloat16 [2048, 6144], P(('depth', 'row'), 'col')
- activation: bfloat16 [2048, 24576], P(('depth', 'col'), 'row')
- weight_grad: float32 [6144, 24576], P('col', ('row', 'depth'))
- bias_grad: float32 [24576], P(('row', 'depth'))
- grad_norm: float32 [], replicated
The draws below stay inside these ranges and needn't reach their ends.
All inputs are finite; a program needn't handle non-finite values.
Results may differ from the reference program's by a relative error of at most 0.01.
Values may be sent and summed in bfloat16 or wider, within the bound.
No kernel may reach another device: no remote copies, remote signals or barrier semaphores. Data moves between devices by JAX's collectives and lax.ppermute only.
A program may use at most 128 MiB of HBM per device.

```python
import math
import jax
import jax.numpy as jnp
from jax import lax

D = 6144
FF = 24576
TOKENS = 2048


def draw_cotangent(key, part):
    key = jax.random.fold_in(key, 7)
    key_base = jax.random.fold_in(key, 1)
    key_rows = jax.random.fold_in(key, 2)
    key_cols = jax.random.fold_in(key, 3)
    col_scale = jnp.exp(math.log(10.0) * jax.random.uniform(key_cols, (1, FF), jnp.float32))
    col_scale = col_scale * jnp.exp(math.log(3.0) * jnp.arange(FF, dtype=jnp.float32) / (FF - 1))
    row_scale = jnp.exp(math.log(10.0) * jax.random.uniform(key_rows, (TOKENS, 1), jnp.float32))
    base_draw = jnp.clip(jax.random.normal(key_base, (TOKENS, FF), jnp.float32), -6.0, 6.0)
    return (base_draw * row_scale * col_scale / 25.0).astype(jnp.bfloat16)


def levels(stream_key, shape, cuts, smallest, largest):
    def one(dim, parts):
        heights = jax.random.uniform(jax.random.fold_in(jax.random.fold_in(stream_key, 6), dim), (parts,), jnp.float32, smallest / len(cuts), largest / len(cuts))
        return jnp.repeat(jnp.exp(heights), shape[dim] // parts).reshape((-1,) + (1,) * (len(shape) - dim - 1))

    loudness = one(*cuts[0])
    for cut in cuts[1:]:
        loudness = loudness * one(*cut)
    return loudness


def noise(stream_key, extent, width, bound, cuts=(), kind=jnp.bfloat16):
    array = jax.random.normal(stream_key, extent, jnp.float32) * width
    if len(cuts) > 0:
        array = levels(stream_key, extent, cuts, -0.22, 0.18) * array
    return jnp.clip(array, min=-bound, max=bound).astype(kind)


def setup_inputs(seed: int = 0) -> dict:
    seeds = jax.random.split(jax.random.key(seed), 5)
    return {
        "tokens": noise(seeds[0], (TOKENS, D), 1.0, 6.0, ((0, 64), (1, 4))),
        "weight": noise(seeds[1], (D, FF), D ** -0.5, 0.078125, ((0, 4), (1, 8))),
        "bias_term": jnp.clip(jax.random.uniform(seeds[2], (FF,), jnp.float32, -1.0, 1.0) * levels(seeds[2], (FF,), ((0, 8),), -0.4, 0.0), -1.0, 1.0),
        "cotangent": draw_cotangent(jax.random.fold_in(seeds[4], 71), 0),
    }


gelu_scale = 0.7978845608
cubic_coef = 0.044715
norm_eps = 1e-06

def gelu_parts(preact):
    inside_term = gelu_scale * (preact + cubic_coef * preact * preact * preact)
    tanh_term = jnp.tanh(inside_term)
    activation = 0.5 * preact * (1.0 + tanh_term)
    slope_term = 0.5 * (1.0 + tanh_term) + 0.5 * preact * (1.0 - tanh_term * tanh_term) * gelu_scale * (1.0 + 3.0 * cubic_coef * preact * preact)
    return (activation, slope_term)

def reference(tokens, weight, bias_term, cotangent):
    preact = jnp.dot(tokens, weight, preferred_element_type=jnp.float32) + bias_term
    activation, slope_term = gelu_parts(preact)
    hidden_out = activation.astype(jnp.bfloat16)
    grad_hidden = (cotangent.astype(jnp.float32) * slope_term).astype(jnp.bfloat16)
    input_grad = jnp.dot(grad_hidden, weight.T, preferred_element_type=jnp.float32).astype(jnp.bfloat16)
    raw_weight = jnp.dot(tokens.T, grad_hidden, preferred_element_type=jnp.float32)
    raw_bias = lax.optimization_barrier(jnp.sum(grad_hidden.astype(jnp.float32), axis=0))
    total_sq = jnp.sum(raw_weight * raw_weight) + jnp.sum(raw_bias * raw_bias)
    grad_norm = jnp.sqrt(total_sq + norm_eps)
    factor = jnp.minimum(1.0, math.sqrt(D * FF) / grad_norm)
    return (input_grad, hidden_out, raw_weight * factor, raw_bias * factor, grad_norm)
```

```python
import math

import jax
import jax.numpy as jnp
from jax import lax
from jax.sharding import PartitionSpec as P

D = 6144
FF = 24576


gelu_scale = 0.7978845608
cubic_coef = 0.044715
norm_eps = 1e-06


def gelu_parts(preact):
    inside_term = gelu_scale * (preact + cubic_coef * preact * preact * preact)
    tanh_term = jnp.tanh(inside_term)
    activation = 0.5 * preact * (1.0 + tanh_term)
    slope_term = 0.5 * (1.0 + tanh_term) + 0.5 * preact * (
        1.0 - tanh_term * tanh_term
    ) * gelu_scale * (1.0 + 3.0 * cubic_coef * preact * preact)
    return (activation, slope_term)


def sum_axis(value, axis):
    n = lax.axis_size(axis)
    tiles = jnp.broadcast_to(value, (n, 8, 128))
    got = lax.all_to_all(tiles, axis, split_axis=0, concat_axis=0, tiled=True)
    return jnp.sum(got[:, 0, 0])


def local(tokens, weight, bias_term, cotangent):
    n_row = lax.axis_size("row")
    n_col = lax.axis_size("col")
    n_depth = lax.axis_size("depth")
    row_index = lax.axis_index("row")
    col_index = lax.axis_index("col")
    core = row_index % 2
    ff = weight.shape[1]
    feat = weight.shape[0]
    share = cotangent.shape[0]
    block_ff = ff // n_depth

    slice_x = lax.all_gather(tokens, "row", axis=0, tiled=True)
    half_rows = slice_x.shape[0] // 2
    half = lax.dynamic_slice_in_dim(slice_x, core * half_rows, half_rows, axis=0)
    mine = lax.all_gather(half, "depth", axis=0, tiled=True)
    swap = [(i, i ^ 1) for i in range(n_row)]
    other = lax.ppermute(mine, "row", swap)

    partial = jnp.dot(slice_x, weight, preferred_element_type=jnp.float32).astype(jnp.bfloat16)
    parts = lax.all_to_all(
        partial.reshape(n_col, share, ff), "col", split_axis=0, concat_axis=0, tiled=True
    )
    preact = jnp.sum(parts.astype(jnp.float32), axis=0) + bias_term
    activation, slope_term = gelu_parts(preact)
    grad_share = (cotangent.astype(jnp.float32) * slope_term).astype(jnp.bfloat16)
    hidden_out = activation.astype(jnp.bfloat16)

    columns = lax.all_to_all(
        grad_share.reshape(share, n_depth, block_ff).transpose(1, 0, 2),
        "depth",
        split_axis=0,
        concat_axis=0,
        tiled=True,
    )
    ordered = lax.all_gather(columns, "col", axis=0, tiled=False)
    grad_slice = lax.all_gather(grad_share, "col", axis=0, tiled=True)

    input_part = lax.dot_general(
        grad_slice, weight, (((1,), (1,)), ((), ())), preferred_element_type=jnp.float32
    )
    input_grad = lax.psum_scatter(input_part, "row", scatter_dimension=0, tiled=True).astype(
        jnp.bfloat16
    )

    pair = n_col // 2
    g_mine = lax.dynamic_slice_in_dim(ordered, core * pair, pair, axis=0)
    g_other = lax.dynamic_slice_in_dim(ordered, (1 - core) * pair, pair, axis=0)

    def meet(t, g):
        t = t.reshape(n_depth, pair, share, feat)
        t = t.transpose(1, 0, 2, 3).reshape(-1, feat)
        g = g.reshape(-1, block_ff)
        return lax.dot_general(t, g, (((0,), (0,)), ((), ())), preferred_element_type=jnp.float32)

    weight_grad = meet(mine, g_mine) + meet(other, g_other)
    bias_grad = jnp.sum(ordered.astype(jnp.float32), axis=(0, 1, 2))
    first_col = (col_index == 0).astype(jnp.float32)
    local_sq = jnp.sum(weight_grad * weight_grad) + first_col * jnp.sum(bias_grad * bias_grad)
    total_sq = sum_axis(sum_axis(sum_axis(local_sq, "row"), "col"), "depth")
    grad_norm = jnp.sqrt(total_sq + norm_eps)
    factor = jnp.minimum(1.0, math.sqrt(D * FF) / grad_norm)
    return (input_grad, hidden_out, weight_grad * factor, bias_grad * factor, grad_norm)


def solution(mesh):
    in_specs = (P(("depth", "row"), "col"), P("col", "row"), P("row"), P(("depth", "col"), "row"))
    out_specs = (
        P(("depth", "row"), "col"),
        P(("depth", "col"), "row"),
        P("col", ("row", "depth")),
        P(("row", "depth")),
        P(),
    )
    return jax.shard_map(local, mesh=mesh, in_specs=in_specs, out_specs=out_specs, check_vma=False)
```

```python
import math

import jax
import jax.numpy as jnp
from jax import lax
from jax.sharding import PartitionSpec as P

D = 6144
FF = 24576

BF = jnp.bfloat16
F32 = jnp.float32

gelu_scale = 0.7978845608
cubic_coef = 0.044715
norm_eps = 1e-06


def gelu_parts(preact):
    inside_term = gelu_scale * (preact + cubic_coef * preact * preact * preact)
    tanh_term = jnp.tanh(inside_term)
    activation = 0.5 * preact * (1.0 + tanh_term)
    slope_term = 0.5 * (1.0 + tanh_term) + 0.5 * preact * (
        1.0 - tanh_term * tanh_term
    ) * gelu_scale * (1.0 + 3.0 * cubic_coef * preact * preact)
    return (activation, slope_term)


def sum_axes(value, axes):
    n = lax.axis_size(axes)
    tiles = jnp.broadcast_to(value, (n, 1, 128))
    got = lax.all_to_all(tiles, axes, split_axis=0, concat_axis=0, tiled=True)
    return jnp.sum(got[:, 0, 0])


def shift_row(value, k):
    n = lax.axis_size("row")
    return lax.ppermute(value, "row", [(i, (i + 2 * k) % n) for i in range(n)])


def swap_core(value):
    n = lax.axis_size("row")
    return lax.ppermute(value, "row", [(i, i ^ 1) for i in range(n)])


def shift_col(value, k):
    n = lax.axis_size("col")
    return lax.ppermute(value, "col", [(i, (i + k) % n) for i in range(n)])


def add_bf(a, b):
    return (a.astype(F32) + b.astype(F32)).astype(BF)


def pick(stack, index):
    return lax.dynamic_index_in_dim(stack, index, 0, keepdims=False)


REL = (2, 1, 3, 0)


def local(tokens, weight, bias_term, cotangent):
    n_col = lax.axis_size("col")
    n_depth = lax.axis_size("depth")
    row_index = lax.axis_index("row")
    col = lax.axis_index("col")
    core = row_index % 2
    y = row_index // 2
    feat, ff = weight.shape
    share = cotangent.shape[0]
    block_ff = ff // n_depth
    tok = tokens.shape[0]
    half_feat = feat // 2
    half_ff = ff // 2

    got = [tokens] + [shift_row(tokens, k) for k in (1, 2, 3)]
    stack = jnp.stack(got)
    mine = jnp.stack([pick(stack, (y - col - k) % 4) for k in REL])
    other = swap_core(mine)
    first = jnp.where(core == 0, mine, other)
    second = jnp.where(core == 0, other, mine)
    slice_x = jnp.stack([first, second], axis=1).reshape(n_col * share, feat)

    half = lax.dynamic_slice_in_dim(slice_x, core * half_feat, half_feat, axis=1)
    all_mine = lax.all_gather(half, "depth", axis=0, tiled=False)
    all_other = swap_core(all_mine)

    p1 = jnp.dot(slice_x, weight[:, :half_ff], preferred_element_type=F32).astype(BF)
    p1 = p1.reshape(n_col, share, half_ff)
    s1 = shift_col(p1[0], 1)
    s2 = shift_col(p1[2], 3)
    p2 = jnp.dot(slice_x, weight[:, half_ff:], preferred_element_type=F32).astype(BF)
    p2 = p2.reshape(n_col, share, half_ff)
    s3 = shift_col(p2[0], 3)
    s4 = shift_col(p2[1], 1)
    s5 = shift_col(add_bf(s1, p1[1]), 1)
    s6 = shift_col(add_bf(s3, p2[2]), 3)
    o1 = p1[3].astype(F32) + s5.astype(F32) + s2.astype(F32)
    o2 = p2[3].astype(F32) + s6.astype(F32) + s4.astype(F32)
    preact = jnp.concatenate([o1, o2], axis=1) + bias_term
    activation, slope_term = gelu_parts(preact)
    grad_share = (cotangent.astype(F32) * slope_term).astype(BF)
    hidden_out = activation.astype(BF)

    columns = lax.all_to_all(
        grad_share.reshape(share, n_depth, block_ff).transpose(1, 0, 2),
        "depth",
        split_axis=0,
        concat_axis=0,
        tiled=True,
    )

    b1 = shift_col(grad_share, 1)
    b3 = shift_col(grad_share, 3)
    b2 = shift_col(grad_share, 2)
    grad_slice = jnp.concatenate([b2, b3, b1, grad_share], axis=0)
    input_part = lax.dot_general(
        grad_slice, weight, (((1,), (1,)), ((), ())), preferred_element_type=F32
    ).reshape(n_col, 2, tok, feat)
    keep = lax.dynamic_index_in_dim(input_part, core, 1, keepdims=False)
    send = lax.dynamic_index_in_dim(input_part, 1 - core, 1, keepdims=False).astype(BF)
    chip = keep + swap_core(send).astype(F32)

    def rel_pos(k):
        d = (y + k - col) % 4
        return jnp.where(d == 2, 0, jnp.where(d == 1, 1, jnp.where(d == 3, 2, 3)))

    input_grad = pick(chip, rel_pos(0))
    for k in (1, 3, 2):
        input_grad = input_grad + shift_row(pick(chip, rel_pos(k)).astype(BF), k).astype(F32)
    input_grad = input_grad.astype(BF)

    hz = n_depth // 2
    lo, hi = columns[:hz], columns[hz:]
    a1 = shift_col(lo, 1)
    d1 = shift_col(hi, 3)
    a2 = shift_col(hi, 1)
    d2 = shift_col(lo, 3)
    a3 = shift_col(a1, 1)
    d3 = shift_col(d1, 3)
    blocks = {
        0: columns,
        3: jnp.concatenate([a1, a2], axis=0),
        1: jnp.concatenate([d2, d1], axis=0),
        2: jnp.concatenate([a3, d3], axis=0),
    }

    def meet(t, k):
        i = REL.index(k)
        return lax.dot_general(
            t[:, i * share : (i + 1) * share],
            blocks[k],
            (((0, 1), (0, 1)), ((), ())),
            preferred_element_type=F32,
        )

    raw_mine = meet(all_mine, 0) + meet(all_mine, 3) + meet(all_mine, 1) + meet(all_mine, 2)
    raw_other = meet(all_other, 0) + meet(all_other, 3) + meet(all_other, 1) + meet(all_other, 2)
    raw_bias = sum(jnp.sum(g.astype(F32), axis=(0, 1)) for g in blocks.values())
    first_col = (col == 0).astype(F32)
    local_sq = (
        jnp.sum(raw_mine * raw_mine)
        + jnp.sum(raw_other * raw_other)
        + first_col * jnp.sum(raw_bias * raw_bias)
    )
    total_sq = sum_axes(sum_axes(local_sq, ("row", "col")), "depth")
    grad_norm = jnp.sqrt(total_sq + norm_eps)
    factor = jnp.minimum(1.0, math.sqrt(D * FF) / grad_norm)
    weight_grad = jnp.concatenate(
        [
            jnp.where(core == 0, raw_mine, raw_other) * factor,
            jnp.where(core == 0, raw_other, raw_mine) * factor,
        ],
        axis=0,
    )
    return (input_grad, hidden_out, weight_grad, raw_bias * factor, grad_norm)


def solution(mesh):
    in_specs = (P(("depth", "row"), "col"), P("col", "row"), P("row"), P(("depth", "col"), "row"))
    out_specs = (
        P(("depth", "row"), "col"),
        P(("depth", "col"), "row"),
        P("col", ("row", "depth")),
        P(("row", "depth")),
        P(),
    )
    return jax.shard_map(local, mesh=mesh, in_specs=in_specs, out_specs=out_specs, check_vma=False)
```

```python
import math

import jax
import jax.numpy as jnp
from jax import lax
from jax.experimental import pallas as pl
from jax.experimental.pallas import tpu as pltpu
from jax.sharding import PartitionSpec as P

D = 6144
FF = 24576

BF = jnp.bfloat16
F32 = jnp.float32
LANES = 128

gelu_scale = 0.7978845608
cubic_coef = 0.044715
norm_eps = 1e-06


def gelu_parts(preact):
    inside_term = gelu_scale * (preact + cubic_coef * preact * preact * preact)
    tanh_term = jnp.tanh(inside_term)
    activation = 0.5 * preact * (1.0 + tanh_term)
    slope_term = 0.5 * (1.0 + tanh_term) + 0.5 * preact * (
        1.0 - tanh_term * tanh_term
    ) * gelu_scale * (1.0 + 3.0 * cubic_coef * preact * preact)
    return (activation, slope_term)


def shift_row(value, k):
    n = lax.axis_size("row")
    return lax.ppermute(value, "row", [(i, (i + 2 * k) % n) for i in range(n)])


def swap_core(value):
    n = lax.axis_size("row")
    return lax.ppermute(value, "row", [(i, i ^ 1) for i in range(n)])


def shift_col(value, k):
    n = lax.axis_size("col")
    return lax.ppermute(value, "col", [(i, (i + k) % n) for i in range(n)])


def shift_depth(value, k):
    n = lax.axis_size("depth")
    return lax.ppermute(value, "depth", [(i, (i + k) % n) for i in range(n)])


def after(value, *others):
    return lax.optimization_barrier((value, *others))[0]


def add_bf(a, b):
    return (a.astype(F32) + b.astype(F32)).astype(BF)


def pick(stack, index):
    return lax.dynamic_index_in_dim(stack, index, 0, keepdims=False)


def choose(options, index):
    res = options[-1]
    for i in range(len(options) - 1):
        res = jnp.where(index == i, options[i], res)
    return res


def stack_kernel(*refs):
    *srcs, dst, held, sems = refs
    n_share = held.shape[1]
    ins, outs, low = [], [], 0
    for i, src in enumerate(srcs):
        size = src.shape[0]
        slot = held.at[low // n_share, low % n_share : low % n_share + size]
        out = dst.at[low // n_share, low % n_share : low % n_share + size]
        ins.append(pltpu.make_async_copy(src, slot, sems.at[0, i]))
        outs.append(pltpu.make_async_copy(slot, out, sems.at[1, i]))
        low += size
    for c in ins:
        c.start()
    for c, d in zip(ins, outs):
        c.wait()
        d.start()
    for d in outs:
        d.wait()


def stack_up(pieces):
    one = pieces[0]
    shape = (sum(p.shape[0] for p in pieces) // one.shape[0],) + one.shape
    return pl.pallas_call(
        stack_kernel,
        in_specs=[pl.BlockSpec(memory_space=pl.ANY)] * len(pieces),
        out_specs=pl.BlockSpec(memory_space=pl.ANY),
        out_shape=jax.ShapeDtypeStruct(shape, one.dtype),
        scratch_shapes=[
            pltpu.VMEM(shape, one.dtype),
            pltpu.SemaphoreType.DMA((2, len(pieces))),
        ],
        compiler_params=pltpu.CompilerParams(vmem_limit_bytes=56 * 2**20),
        cost_estimate=pl.CostEstimate(
            flops=0, bytes_accessed=4 * math.prod(shape), transcendentals=0
        ),
        name="stack_up",
    )(*pieces)


REL = (2, 1, 3, 0)


def grad_step(t_mine, t_other, pieces, acc, depth, first_col=None):
    n_depth, n_share, rows, feat = t_mine.shape
    block_ff = pieces[0][1][0].shape[-1]
    width = 512
    kdim = n_depth * rows
    n_p = len(pieces)
    counts = [len(p[1]) for p in pieces]
    flat = [b for p in pieces for b in p[1]]
    final = first_col is not None
    have = acc is not None

    def body(*refs):
        refs = list(refs)
        depth_ref = refs.pop(0)
        first_ref = refs.pop(0) if final else None
        t_refs = [(refs.pop(0), refs.pop(0)) for _ in range(n_p)]
        g_refs = [refs.pop(0) for _ in flat]
        acc_ref, bias_in = (refs.pop(0), refs.pop(0)) if have else (None, None)
        out_ref, bias_out = refs.pop(0), refs.pop(0)
        sq_out = refs.pop(0) if final else None
        stage, gt = refs.pop(0), refs.pop(0)
        total = refs.pop(0) if final else None
        step = pl.program_id(0)

        @pl.when(step == 0)
        def _():
            me = depth_ref[0]
            bias = jnp.zeros((1, block_ff), F32)
            if have:
                bias = bias_in[...]
            at = 0
            for i in range(n_p):
                low = 0
                for _ in range(counts[i]):
                    g = g_refs[at]
                    at += 1
                    size = g.shape[0]
                    stage[low : low + size] = g[...]
                    low += size
                whole = stage[...].reshape(n_depth * 2 * rows, block_ff)
                bias = bias + jnp.sum(whole.astype(F32), axis=0, keepdims=True)
                for half in range(2):
                    parts = []
                    for d in range(n_depth):
                        z = lax.rem(me + n_depth - d, n_depth)
                        parts.append(stage[z, half * rows : (half + 1) * rows, :])
                    gt[2 * i + half] = jnp.concatenate(parts, axis=0).T
            bias_out[...] = bias

        res = acc_ref[...] if have else None
        for i in range(n_p):
            for half in range(2):
                t = t_refs[i][half][...].reshape(kdim, width)
                one = jnp.dot(gt[2 * i + half], t, preferred_element_type=F32)
                res = one if res is None else res + one
        out_ref[...] = res
        if final:
            here = jnp.sum(res * res, keepdims=True)

            @pl.when(step == 0)
            def _():
                b = bias_out[...]
                total[...] = here + first_ref[0] * jnp.sum(b * b, keepdims=True)

            @pl.when(step > 0)
            def _():
                total[...] += here

            sq_out[...] = jnp.broadcast_to(total[...].reshape(1, 1, 1), sq_out.shape)

    smem = pl.BlockSpec(memory_space=pltpu.SMEM)

    def whole_spec(shape):
        return pl.BlockSpec(shape, lambda j: (0,) * len(shape))

    def t_spec(pos):
        return pl.BlockSpec((n_depth, 1, rows, width), lambda j: (0, pos, 0, j))

    acc_spec = pl.BlockSpec((block_ff, width), lambda j: (0, j))
    bias_spec = whole_spec((1, block_ff))
    ins = [depth] + ([first_col] if final else [])
    specs = [smem] * len(ins)
    for pos, _ in pieces:
        ins += [t_mine, t_other]
        specs += [t_spec(pos)] * 2
    ins += flat
    specs += [whole_spec(b.shape) for b in flat]
    if have:
        ins += list(acc)
        specs += [acc_spec, bias_spec]
    out_shape = [
        jax.ShapeDtypeStruct((block_ff, feat), F32),
        jax.ShapeDtypeStruct((1, block_ff), F32),
    ]
    out_specs = [acc_spec, bias_spec]
    scratch = [
        pltpu.VMEM((n_depth, 2 * rows, block_ff), BF),
        pltpu.VMEM((2 * n_p, block_ff, kdim), BF),
    ]
    if final:
        n_sq = lax.axis_size(("row", "col"))
        out_shape.append(jax.ShapeDtypeStruct((n_sq, 1, LANES), F32))
        out_specs.append(whole_spec((n_sq, 1, LANES)))
        scratch.append(pltpu.VMEM((1, 1), F32))
    return pl.pallas_call(
        body,
        grid=(feat // width,),
        in_specs=specs,
        out_specs=out_specs,
        out_shape=out_shape,
        scratch_shapes=scratch,
        compiler_params=pltpu.CompilerParams(vmem_limit_bytes=12 * 2**20),
        cost_estimate=pl.CostEstimate(
            flops=n_p * 4 * kdim * block_ff * feat,
            bytes_accessed=n_p * 4 * kdim * feat + 8 * block_ff * feat,
            transcendentals=0,
        ),
        name="grad_step",
    )(*ins)


def clip(parts, raw, bias):
    block_ff, feat = raw.shape
    width = 256

    def body(p, r, b, o, ob, on):
        total = jnp.sum(p[...], axis=0)[:, :1]
        norm = jnp.sqrt(total + norm_eps)
        factor = jnp.minimum(1.0, math.sqrt(D * FF) / norm)
        o[...] = r[...].T * factor
        ob[...] = (b[...] * factor).reshape(block_ff)
        on[0] = norm[0, 0]

    def whole_spec(shape):
        return pl.BlockSpec(shape, lambda j: (0,) * len(shape))

    return pl.pallas_call(
        body,
        grid=(feat // width,),
        in_specs=[
            whole_spec(parts.shape),
            pl.BlockSpec((block_ff, width), lambda j: (0, j)),
            whole_spec((1, block_ff)),
        ],
        out_specs=[
            pl.BlockSpec((width, block_ff), lambda j: (j, 0)),
            whole_spec((block_ff,)),
            pl.BlockSpec(memory_space=pltpu.SMEM),
        ],
        out_shape=[
            jax.ShapeDtypeStruct((feat, block_ff), F32),
            jax.ShapeDtypeStruct((block_ff,), F32),
            jax.ShapeDtypeStruct((1,), F32),
        ],
        compiler_params=pltpu.CompilerParams(vmem_limit_bytes=4 * 2**20),
        name="clip",
    )(parts, raw, bias)


def exchange(value, axes):
    return lax.all_to_all(value, axes, split_axis=0, concat_axis=0, tiled=True)


def local(tokens, weight, bias_term, cotangent):
    n_col = lax.axis_size("col")
    n_depth = lax.axis_size("depth")
    row_index = lax.axis_index("row")
    col = lax.axis_index("col")
    depth = lax.axis_index("depth")
    core = row_index % 2
    y = row_index // 2
    feat, ff = weight.shape
    share = cotangent.shape[0]
    block_ff = ff // n_depth
    tok = tokens.shape[0]
    half_ff = ff // 2

    def own_first(v):
        return jnp.where(core == 0, v, jnp.concatenate([v[tok:], v[:tok]], axis=0))

    got = [tokens] + [shift_row(tokens, k) for k in (1, 2, 3)]
    mine = jnp.stack([choose(got, (y - col - k) % 4) for k in REL])
    other = swap_core(mine)
    slice_x = jnp.concatenate([mine, other], axis=1).reshape(n_col * share, feat)

    up1, dn1 = shift_depth(mine, 1), shift_depth(mine, n_depth - 1)
    up2, dn2 = shift_depth(up1, 1), shift_depth(dn1, n_depth - 1)
    up3, dn3 = shift_depth(up2, 1), shift_depth(dn2, n_depth - 1)
    up4 = shift_depth(up3[: n_col // 2], 1)
    dn4 = shift_depth(dn3[n_col // 2 :], n_depth - 1)

    p1 = jnp.dot(slice_x, weight[:, :half_ff], preferred_element_type=F32).astype(BF)
    p1 = p1.reshape(n_col, share, half_ff)
    p2 = jnp.dot(slice_x, weight[:, half_ff:], preferred_element_type=F32).astype(BF)
    p2 = p2.reshape(n_col, share, half_ff)
    s1 = shift_col(p1[0], 1)
    s3 = shift_col(p2[0], 3)
    s5 = shift_col(jnp.concatenate([add_bf(s1, p1[1]), p2[1]], axis=1), 1)
    s6 = shift_col(jnp.concatenate([p1[2], add_bf(s3, p2[2])], axis=1), 3)
    o1 = p1[3].astype(F32) + s5[:, :half_ff].astype(F32) + s6[:, :half_ff].astype(F32)
    o2 = p2[3].astype(F32) + s6[:, half_ff:].astype(F32) + s5[:, half_ff:].astype(F32)
    preact = jnp.concatenate([o1, o2], axis=1) + bias_term
    activation, slope_term = gelu_parts(preact)
    grad_share = (own_first(cotangent).astype(F32) * slope_term).astype(BF)
    hidden_out = own_first(activation.astype(BF))

    later = after(grad_share, up3, dn3)
    b1 = shift_col(later, 1)
    b3 = shift_col(later, 3)
    b2 = shift_col(b1[:tok], 1)
    b4 = shift_col(b3[tok:], 3)
    columns = exchange(after(grad_share, up2, dn2).reshape(share, n_depth, block_ff).transpose(1, 0, 2), "depth")

    columns, b1, b2, b3, b4 = lax.optimization_barrier((columns, b1, b2, b3, b4))
    t_mine = stack_up([after(mine, columns), up1, up2, up3, up4, dn4, dn3, dn2, dn1])
    t_other = swap_core(t_mine)

    hz = n_depth // 2
    a1 = shift_col(columns, 1)
    d1 = shift_col(columns, 3)
    depth_arr = depth.astype(jnp.int32).reshape(1)
    at = {k: REL.index(k) for k in REL}
    grad_slice = jnp.concatenate([b2, b4, b3, b1, grad_share], axis=0)
    input_part = lax.dot_general(
        grad_slice, weight, (((1,), (1,)), ((), ())), preferred_element_type=F32
    ).reshape(n_col, 2, tok, feat)
    a1, d1, input_part = lax.optimization_barrier((a1, d1, input_part))
    a3 = shift_col(a1[:hz], 1)
    d3 = shift_col(d1[hz:], 3)
    acc = grad_step(
        t_mine,
        t_other,
        [(at[0], [columns]), (at[3], [a1]), (at[1], [d1])],
        None,
        depth_arr,
    )
    chip = input_part[:, 0] + swap_core(input_part[:, 1].astype(BF)).astype(F32)

    def rel_pos(k):
        d = (y + k - col) % 4
        return jnp.where(d == 2, 0, jnp.where(d == 1, 1, jnp.where(d == 3, 2, 3)))

    came = [shift_row(pick(chip, rel_pos(k)).astype(BF), k) for k in (1, 3, 2)]
    a3, d3, acc, came = lax.optimization_barrier((a3, d3, acc, came))
    first_col = (col == 0).astype(F32).reshape(1)
    raw, raw_bias, squares = grad_step(
        t_mine, t_other, [(at[2], [a3, d3])], acc, depth_arr, first_col
    )

    input_grad = pick(chip, rel_pos(0))
    for part in came:
        input_grad = input_grad + part.astype(F32)
    input_grad = input_grad.astype(BF)

    squares = jnp.sum(exchange(squares, ("row", "col")), axis=0, keepdims=True)
    squares = jnp.broadcast_to(squares, (n_depth,) + squares.shape[1:])
    weight_grad, bias_grad, grad_norm = clip(exchange(squares, "depth"), raw, raw_bias)
    return (input_grad, hidden_out, weight_grad, bias_grad, grad_norm[0])


def solution(mesh):
    in_specs = (P(("depth", "row"), "col"), P("col", "row"), P("row"), P(("depth", "col"), "row"))
    out_specs = (
        P(("depth", "row"), "col"),
        P(("depth", "col"), "row"),
        P("col", ("row", "depth")),
        P(("row", "depth")),
        P(),
    )
    return jax.shard_map(local, mesh=mesh, in_specs=in_specs, out_specs=out_specs, check_vma=False)
```

```python
import math

import jax
import jax.numpy as jnp
from jax import lax
from jax.experimental import pallas as pl
from jax.experimental.pallas import tpu as pltpu
from jax.sharding import PartitionSpec as P

D = 6144
FF = 24576

BF = jnp.bfloat16
F32 = jnp.float32
LANES = 128

gelu_scale = 0.7978845608
cubic_coef = 0.044715
norm_eps = 1e-06


def gelu_parts(preact):
    inside_term = gelu_scale * (preact + cubic_coef * preact * preact * preact)
    tanh_term = jnp.tanh(inside_term)
    activation = 0.5 * preact * (1.0 + tanh_term)
    slope_term = 0.5 * (1.0 + tanh_term) + 0.5 * preact * (
        1.0 - tanh_term * tanh_term
    ) * gelu_scale * (1.0 + 3.0 * cubic_coef * preact * preact)
    return (activation, slope_term)


def shift_row(value, k):
    n = lax.axis_size("row")
    return lax.ppermute(value, "row", [(i, (i + 2 * k) % n) for i in range(n)])


def swap_core(value):
    n = lax.axis_size("row")
    return lax.ppermute(value, "row", [(i, i ^ 1) for i in range(n)])


def shift_col(value, k):
    n = lax.axis_size("col")
    return lax.ppermute(value, "col", [(i, (i + k) % n) for i in range(n)])


def shift_depth(value, k):
    n = lax.axis_size("depth")
    return lax.ppermute(value, "depth", [(i, (i + k) % n) for i in range(n)])


def after(value, *others):
    return lax.optimization_barrier((value, *others))[0]


def add_bf(a, b):
    return (a.astype(F32) + b.astype(F32)).astype(BF)


def pick(stack, index):
    return lax.dynamic_index_in_dim(stack, index, 0, keepdims=False)


def choose(options, index):
    res = options[-1]
    for i in range(len(options) - 1):
        res = jnp.where(index == i, options[i], res)
    return res


def stack_kernel(*refs):
    *srcs, dst, held, sems = refs
    n_share = held.shape[1]
    ins, outs, low = [], [], 0
    for i, src in enumerate(srcs):
        size = src.shape[0]
        slot = held.at[low // n_share, low % n_share : low % n_share + size]
        out = dst.at[low // n_share, low % n_share : low % n_share + size]
        ins.append(pltpu.make_async_copy(src, slot, sems.at[0, i]))
        outs.append(pltpu.make_async_copy(slot, out, sems.at[1, i]))
        low += size
    for c in ins:
        c.start()
    for c, d in zip(ins, outs):
        c.wait()
        d.start()
    for d in outs:
        d.wait()


def stack_up(pieces):
    one = pieces[0]
    shape = (sum(p.shape[0] for p in pieces) // one.shape[0],) + one.shape
    return pl.pallas_call(
        stack_kernel,
        in_specs=[pl.BlockSpec(memory_space=pl.ANY)] * len(pieces),
        out_specs=pl.BlockSpec(memory_space=pl.ANY),
        out_shape=jax.ShapeDtypeStruct(shape, one.dtype),
        scratch_shapes=[
            pltpu.VMEM(shape, one.dtype),
            pltpu.SemaphoreType.DMA((2, len(pieces))),
        ],
        compiler_params=pltpu.CompilerParams(vmem_limit_bytes=56 * 2**20),
        cost_estimate=pl.CostEstimate(
            flops=0, bytes_accessed=4 * math.prod(shape), transcendentals=0
        ),
        name="stack_up",
    )(*pieces)


REL = (2, 1, 3, 0)


def grad_step(t_mine, t_other, pieces, acc, depth, first_col=None):
    n_depth, n_share, rows, feat = t_mine.shape
    block_ff = pieces[0][1][0].shape[-1]
    width = 512
    kdim = n_depth * rows
    n_p = len(pieces)
    counts = [len(p[1]) for p in pieces]
    flat = [b for p in pieces for b in p[1]]
    final = first_col is not None
    have = acc is not None

    def body(*refs):
        refs = list(refs)
        depth_ref = refs.pop(0)
        first_ref = refs.pop(0) if final else None
        t_refs = [(refs.pop(0), refs.pop(0)) for _ in range(n_p)]
        g_refs = [refs.pop(0) for _ in flat]
        acc_ref, bias_in = (refs.pop(0), refs.pop(0)) if have else (None, None)
        out_ref, bias_out = refs.pop(0), refs.pop(0)
        sq_out = refs.pop(0) if final else None
        stage, gt = refs.pop(0), refs.pop(0)
        total = refs.pop(0) if final else None
        step = pl.program_id(0)

        @pl.when(step == 0)
        def _():
            me = depth_ref[0]
            bias = jnp.zeros((1, block_ff), F32)
            if have:
                bias = bias_in[...]
            at = 0
            for i in range(n_p):
                low = 0
                for _ in range(counts[i]):
                    g = g_refs[at]
                    at += 1
                    size = g.shape[0]
                    stage[low : low + size] = g[...]
                    low += size
                whole = stage[...].reshape(n_depth * 2 * rows, block_ff)
                bias = bias + jnp.sum(whole.astype(F32), axis=0, keepdims=True)
                for half in range(2):
                    parts = []
                    for d in range(n_depth):
                        z = lax.rem(me + n_depth - d, n_depth)
                        parts.append(stage[z, half * rows : (half + 1) * rows, :])
                    gt[2 * i + half] = jnp.concatenate(parts, axis=0).T
            bias_out[...] = bias

        res = acc_ref[...] if have else None
        for i in range(n_p):
            for half in range(2):
                t = t_refs[i][half][...].reshape(kdim, width)
                one = jnp.dot(gt[2 * i + half], t, preferred_element_type=F32)
                res = one if res is None else res + one
        out_ref[...] = res
        if final:
            here = jnp.sum(res * res, keepdims=True)

            @pl.when(step == 0)
            def _():
                b = bias_out[...]
                total[...] = here + first_ref[0] * jnp.sum(b * b, keepdims=True)

            @pl.when(step > 0)
            def _():
                total[...] += here

            sq_out[...] = jnp.broadcast_to(total[...].reshape(1, 1, 1), sq_out.shape)

    smem = pl.BlockSpec(memory_space=pltpu.SMEM)

    def whole_spec(shape):
        return pl.BlockSpec(shape, lambda j: (0,) * len(shape))

    def t_spec(pos):
        return pl.BlockSpec((n_depth, 1, rows, width), lambda j: (0, pos, 0, j))

    acc_spec = pl.BlockSpec((block_ff, width), lambda j: (0, j))
    bias_spec = whole_spec((1, block_ff))
    ins = [depth] + ([first_col] if final else [])
    specs = [smem] * len(ins)
    for pos, _ in pieces:
        ins += [t_mine, t_other]
        specs += [t_spec(pos)] * 2
    ins += flat
    specs += [whole_spec(b.shape) for b in flat]
    if have:
        ins += list(acc)
        specs += [acc_spec, bias_spec]
    out_shape = [
        jax.ShapeDtypeStruct((block_ff, feat), F32),
        jax.ShapeDtypeStruct((1, block_ff), F32),
    ]
    out_specs = [acc_spec, bias_spec]
    scratch = [
        pltpu.VMEM((n_depth, 2 * rows, block_ff), BF),
        pltpu.VMEM((2 * n_p, block_ff, kdim), BF),
    ]
    if final:
        n_sq = lax.axis_size(("row", "col"))
        out_shape.append(jax.ShapeDtypeStruct((n_sq, 1, LANES), F32))
        out_specs.append(whole_spec((n_sq, 1, LANES)))
        scratch.append(pltpu.VMEM((1, 1), F32))
    return pl.pallas_call(
        body,
        grid=(feat // width,),
        in_specs=specs,
        out_specs=out_specs,
        out_shape=out_shape,
        scratch_shapes=scratch,
        compiler_params=pltpu.CompilerParams(vmem_limit_bytes=12 * 2**20),
        cost_estimate=pl.CostEstimate(
            flops=n_p * 4 * kdim * block_ff * feat,
            bytes_accessed=n_p * 4 * kdim * feat + 8 * block_ff * feat,
            transcendentals=0,
        ),
        name="grad_step",
    )(*ins)


def clip(parts, raw, bias):
    block_ff, feat = raw.shape
    width = 256

    def body(p, r, b, o, ob, on):
        total = jnp.sum(p[...], axis=0)[:, :1]
        norm = jnp.sqrt(total + norm_eps)
        factor = jnp.minimum(1.0, math.sqrt(D * FF) / norm)
        o[...] = r[...].T * factor
        ob[...] = (b[...] * factor).reshape(block_ff)
        on[0] = norm[0, 0]

    def whole_spec(shape):
        return pl.BlockSpec(shape, lambda j: (0,) * len(shape))

    return pl.pallas_call(
        body,
        grid=(feat // width,),
        in_specs=[
            whole_spec(parts.shape),
            pl.BlockSpec((block_ff, width), lambda j: (0, j)),
            whole_spec((1, block_ff)),
        ],
        out_specs=[
            pl.BlockSpec((width, block_ff), lambda j: (j, 0)),
            whole_spec((block_ff,)),
            pl.BlockSpec(memory_space=pltpu.SMEM),
        ],
        out_shape=[
            jax.ShapeDtypeStruct((feat, block_ff), F32),
            jax.ShapeDtypeStruct((block_ff,), F32),
            jax.ShapeDtypeStruct((1,), F32),
        ],
        compiler_params=pltpu.CompilerParams(vmem_limit_bytes=4 * 2**20),
        name="clip",
    )(parts, raw, bias)


def exchange(value, axes):
    return lax.all_to_all(value, axes, split_axis=0, concat_axis=0, tiled=True)


def local(tokens, weight, bias_term, cotangent):
    n_col = lax.axis_size("col")
    n_depth = lax.axis_size("depth")
    row_index = lax.axis_index("row")
    col = lax.axis_index("col")
    depth = lax.axis_index("depth")
    core = row_index % 2
    y = row_index // 2
    feat, ff = weight.shape
    share = cotangent.shape[0]
    block_ff = ff // n_depth
    tok = tokens.shape[0]
    half_ff = ff // 2

    def own_first(v):
        return jnp.where(core == 0, v, jnp.concatenate([v[tok:], v[:tok]], axis=0))

    got = [tokens] + [shift_row(tokens, k) for k in (1, 2, 3)]
    mine = jnp.stack([choose(got, (y - col - k) % 4) for k in REL])
    other = swap_core(mine)
    slice_x = jnp.concatenate([mine, other], axis=1).reshape(n_col * share, feat)

    up1, dn1 = shift_depth(mine, 1), shift_depth(mine, n_depth - 1)
    up2, dn2 = shift_depth(up1, 1), shift_depth(dn1, n_depth - 1)
    up3, dn3 = shift_depth(up2, 1), shift_depth(dn2, n_depth - 1)
    up4 = shift_depth(up3[: n_col // 2], 1)
    dn4 = shift_depth(dn3[n_col // 2 :], n_depth - 1)

    p1 = jnp.dot(slice_x, weight[:, :half_ff], preferred_element_type=F32).astype(BF)
    p1 = p1.reshape(n_col, share, half_ff)
    p2 = jnp.dot(slice_x, weight[:, half_ff:], preferred_element_type=F32).astype(BF)
    p2 = p2.reshape(n_col, share, half_ff)
    s1 = shift_col(p1[0], 1)
    s3 = shift_col(p2[0], 3)
    s5 = shift_col(jnp.concatenate([add_bf(s1, p1[1]), p2[1]], axis=1), 1)
    s6 = shift_col(jnp.concatenate([p1[2], add_bf(s3, p2[2])], axis=1), 3)
    o1 = p1[3].astype(F32) + s5[:, :half_ff].astype(F32) + s6[:, :half_ff].astype(F32)
    o2 = p2[3].astype(F32) + s6[:, half_ff:].astype(F32) + s5[:, half_ff:].astype(F32)
    preact = jnp.concatenate([o1, o2], axis=1) + bias_term
    activation, slope_term = gelu_parts(preact)
    grad_share = (own_first(cotangent).astype(F32) * slope_term).astype(BF)
    hidden_out = own_first(activation.astype(BF))

    later = after(grad_share, up3, dn3)
    b1 = shift_col(later, 1)
    b3 = shift_col(later, 3)
    b2 = shift_col(b1[:tok], 1)
    b4 = shift_col(b3[tok:], 3)
    columns = exchange(after(grad_share, up2, dn2).reshape(share, n_depth, block_ff).transpose(1, 0, 2), "depth")

    columns, b1, b3 = lax.optimization_barrier((columns, b1, b3))
    t_mine = stack_up([after(mine, columns), up1, up2, up3, up4, dn4, dn3, dn2, dn1])
    t_other = swap_core(t_mine)

    hz = n_depth // 2
    a1 = shift_col(columns, 1)
    d1 = shift_col(columns, 3)
    depth_arr = depth.astype(jnp.int32).reshape(1)
    at = {k: REL.index(k) for k in REL}
    grad_slice = jnp.concatenate([b2, b4, b3, b1, grad_share], axis=0)
    input_part = lax.dot_general(
        grad_slice, weight, (((1,), (1,)), ((), ())), preferred_element_type=F32
    ).reshape(n_col, 2, tok, feat)
    a1, d1, input_part = lax.optimization_barrier((a1, d1, input_part))
    a3 = shift_col(a1[:hz], 1)
    d3 = shift_col(d1[hz:], 3)
    acc = grad_step(
        t_mine,
        t_other,
        [(at[0], [columns]), (at[3], [a1]), (at[1], [d1])],
        None,
        depth_arr,
    )
    chip = input_part[:, 0] + swap_core(input_part[:, 1].astype(BF)).astype(F32)

    def rel_pos(k):
        d = (y + k - col) % 4
        return jnp.where(d == 2, 0, jnp.where(d == 1, 1, jnp.where(d == 3, 2, 3)))

    came = [shift_row(pick(chip, rel_pos(k)).astype(BF), k) for k in (1, 3, 2)]
    a3, d3, acc, came = lax.optimization_barrier((a3, d3, acc, came))
    first_col = (col == 0).astype(F32).reshape(1)
    raw, raw_bias, squares = grad_step(
        t_mine, t_other, [(at[2], [a3, d3])], acc, depth_arr, first_col
    )

    input_grad = pick(chip, rel_pos(0))
    for part in came:
        input_grad = input_grad + part.astype(F32)
    input_grad = input_grad.astype(BF)

    squares = jnp.sum(exchange(squares, ("row", "col")), axis=0, keepdims=True)
    squares = jnp.broadcast_to(squares, (n_depth,) + squares.shape[1:])
    weight_grad, bias_grad, grad_norm = clip(exchange(squares, "depth"), raw, raw_bias)
    return (input_grad, hidden_out, weight_grad, bias_grad, grad_norm[0])


def solution(mesh):
    in_specs = (P(("depth", "row"), "col"), P("col", "row"), P("row"), P(("depth", "col"), "row"))
    out_specs = (
        P(("depth", "row"), "col"),
        P(("depth", "col"), "row"),
        P("col", ("row", "depth")),
        P(("row", "depth")),
        P(),
    )
    return jax.shard_map(local, mesh=mesh, in_specs=in_specs, out_specs=out_specs, check_vma=False)
```

```python
import math

import jax
import jax.numpy as jnp
from jax import lax
from jax.experimental import pallas as pl
from jax.experimental.pallas import tpu as pltpu
from jax.sharding import PartitionSpec as P

D = 6144
FF = 24576

BF = jnp.bfloat16
F32 = jnp.float32
LANES = 128

gelu_scale = 0.7978845608
cubic_coef = 0.044715
norm_eps = 1e-06


def gelu_parts(preact):
    inside_term = gelu_scale * (preact + cubic_coef * preact * preact * preact)
    tanh_term = jnp.tanh(inside_term)
    activation = 0.5 * preact * (1.0 + tanh_term)
    slope_term = 0.5 * (1.0 + tanh_term) + 0.5 * preact * (
        1.0 - tanh_term * tanh_term
    ) * gelu_scale * (1.0 + 3.0 * cubic_coef * preact * preact)
    return (activation, slope_term)


def shift_row(value, k):
    n = lax.axis_size("row")
    return lax.ppermute(value, "row", [(i, (i + 2 * k) % n) for i in range(n)])


def swap_core(value):
    n = lax.axis_size("row")
    return lax.ppermute(value, "row", [(i, i ^ 1) for i in range(n)])


def shift_col(value, k):
    n = lax.axis_size("col")
    return lax.ppermute(value, "col", [(i, (i + k) % n) for i in range(n)])


def shift_depth(value, k):
    n = lax.axis_size("depth")
    return lax.ppermute(value, "depth", [(i, (i + k) % n) for i in range(n)])


def after(value, *others):
    return lax.optimization_barrier((value, *others))[0]


def add_bf(a, b):
    return (a.astype(F32) + b.astype(F32)).astype(BF)


def pick(stack, index):
    return lax.dynamic_index_in_dim(stack, index, 0, keepdims=False)


def choose(options, index):
    res = options[-1]
    for i in range(len(options) - 1):
        res = jnp.where(index == i, options[i], res)
    return res


def stack_kernel(*refs):
    *srcs, dst, held, sems = refs
    n_share = held.shape[1]
    ins, outs, low = [], [], 0
    for i, src in enumerate(srcs):
        size = src.shape[0]
        slot = held.at[low // n_share, low % n_share : low % n_share + size]
        out = dst.at[low // n_share, low % n_share : low % n_share + size]
        ins.append(pltpu.make_async_copy(src, slot, sems.at[0, i]))
        outs.append(pltpu.make_async_copy(slot, out, sems.at[1, i]))
        low += size
    for c in ins:
        c.start()
    for c, d in zip(ins, outs):
        c.wait()
        d.start()
    for d in outs:
        d.wait()


def stack_up(pieces):
    one = pieces[0]
    shape = (sum(p.shape[0] for p in pieces) // one.shape[0],) + one.shape
    return pl.pallas_call(
        stack_kernel,
        in_specs=[pl.BlockSpec(memory_space=pl.ANY)] * len(pieces),
        out_specs=pl.BlockSpec(memory_space=pl.ANY),
        out_shape=jax.ShapeDtypeStruct(shape, one.dtype),
        scratch_shapes=[
            pltpu.VMEM(shape, one.dtype),
            pltpu.SemaphoreType.DMA((2, len(pieces))),
        ],
        compiler_params=pltpu.CompilerParams(vmem_limit_bytes=56 * 2**20),
        cost_estimate=pl.CostEstimate(
            flops=0, bytes_accessed=4 * math.prod(shape), transcendentals=0
        ),
        name="stack_up",
    )(*pieces)


REL = (2, 1, 3, 0)


def grad_step(t_mine, t_other, pieces, acc, depth, first_col=None):
    n_depth, n_share, rows, feat = t_mine.shape
    block_ff = pieces[0][1][0].shape[-1]
    width = 1536
    kdim = n_depth * rows
    n_p = len(pieces)
    counts = [len(p[1]) for p in pieces]
    flat = [b for p in pieces for b in p[1]]
    final = first_col is not None
    have = acc is not None

    def body(*refs):
        refs = list(refs)
        depth_ref = refs.pop(0)
        first_ref = refs.pop(0) if final else None
        t_refs = [(refs.pop(0), refs.pop(0)) for _ in range(n_p)]
        g_refs = [refs.pop(0) for _ in flat]
        acc_ref, bias_in = (refs.pop(0), refs.pop(0)) if have else (None, None)
        out_ref, bias_out = refs.pop(0), refs.pop(0)
        sq_out = refs.pop(0) if final else None
        stage, gt = refs.pop(0), refs.pop(0)
        total = refs.pop(0) if final else None
        step = pl.program_id(0)

        @pl.when(step == 0)
        def _():
            me = depth_ref[0]
            bias = jnp.zeros((1, block_ff), F32)
            if have:
                bias = bias_in[...]
            at = 0
            for i in range(n_p):
                low = 0
                for _ in range(counts[i]):
                    g = g_refs[at]
                    at += 1
                    size = g.shape[0]
                    stage[low : low + size] = g[...]
                    low += size
                whole = stage[...].reshape(n_depth * 2 * rows, block_ff)
                bias = bias + jnp.sum(whole.astype(F32), axis=0, keepdims=True)
                for half in range(2):
                    parts = []
                    for d in range(n_depth):
                        z = lax.rem(me + n_depth - d, n_depth)
                        parts.append(stage[z, half * rows : (half + 1) * rows, :])
                    gt[2 * i + half] = jnp.concatenate(parts, axis=0).T
            bias_out[...] = bias

        res = acc_ref[...] if have else None
        for i in range(n_p):
            for half in range(2):
                t = t_refs[i][half][...].reshape(kdim, width)
                one = jnp.dot(gt[2 * i + half], t, preferred_element_type=F32)
                res = one if res is None else res + one
        out_ref[...] = res
        if final:
            here = jnp.sum(res * res, keepdims=True)

            @pl.when(step == 0)
            def _():
                b = bias_out[...]
                total[...] = here + first_ref[0] * jnp.sum(b * b, keepdims=True)

            @pl.when(step > 0)
            def _():
                total[...] += here

            sq_out[...] = jnp.broadcast_to(total[...].reshape(1, 1, 1), sq_out.shape)

    smem = pl.BlockSpec(memory_space=pltpu.SMEM)

    def whole_spec(shape):
        return pl.BlockSpec(shape, lambda j: (0,) * len(shape))

    def t_spec(pos):
        return pl.BlockSpec((n_depth, 1, rows, width), lambda j: (0, pos, 0, j))

    acc_spec = pl.BlockSpec((block_ff, width), lambda j: (0, j))
    bias_spec = whole_spec((1, block_ff))
    ins = [depth] + ([first_col] if final else [])
    specs = [smem] * len(ins)
    for pos, _ in pieces:
        ins += [t_mine, t_other]
        specs += [t_spec(pos)] * 2
    ins += flat
    specs += [whole_spec(b.shape) for b in flat]
    if have:
        ins += list(acc)
        specs += [acc_spec, bias_spec]
    out_shape = [
        jax.ShapeDtypeStruct((block_ff, feat), F32),
        jax.ShapeDtypeStruct((1, block_ff), F32),
    ]
    out_specs = [acc_spec, bias_spec]
    scratch = [
        pltpu.VMEM((n_depth, 2 * rows, block_ff), BF),
        pltpu.VMEM((2 * n_p, block_ff, kdim), BF),
    ]
    if final:
        n_sq = lax.axis_size(("row", "col"))
        out_shape.append(jax.ShapeDtypeStruct((n_sq, 1, LANES), F32))
        out_specs.append(whole_spec((n_sq, 1, LANES)))
        scratch.append(pltpu.VMEM((1, 1), F32))
    return pl.pallas_call(
        body,
        grid=(feat // width,),
        in_specs=specs,
        out_specs=out_specs,
        out_shape=out_shape,
        scratch_shapes=scratch,
        compiler_params=pltpu.CompilerParams(vmem_limit_bytes=24 * 2**20),
        cost_estimate=pl.CostEstimate(
            flops=n_p * 4 * kdim * block_ff * feat,
            bytes_accessed=n_p * 4 * kdim * feat + 8 * block_ff * feat,
            transcendentals=0,
        ),
        name="grad_step",
    )(*ins)


def clip(parts, raw, bias):
    block_ff, feat = raw.shape
    width = 768

    def body(p, r, b, o, ob, on):
        total = jnp.sum(p[...], axis=0)[:, :1]
        norm = jnp.sqrt(total + norm_eps)
        factor = jnp.minimum(1.0, math.sqrt(D * FF) / norm)
        o[...] = r[...].T * factor
        ob[...] = (b[...] * factor).reshape(block_ff)
        on[0] = norm[0, 0]

    def whole_spec(shape):
        return pl.BlockSpec(shape, lambda j: (0,) * len(shape))

    return pl.pallas_call(
        body,
        grid=(feat // width,),
        in_specs=[
            whole_spec(parts.shape),
            pl.BlockSpec((block_ff, width), lambda j: (0, j)),
            whole_spec((1, block_ff)),
        ],
        out_specs=[
            pl.BlockSpec((width, block_ff), lambda j: (j, 0)),
            whole_spec((block_ff,)),
            pl.BlockSpec(memory_space=pltpu.SMEM),
        ],
        out_shape=[
            jax.ShapeDtypeStruct((feat, block_ff), F32),
            jax.ShapeDtypeStruct((block_ff,), F32),
            jax.ShapeDtypeStruct((1,), F32),
        ],
        compiler_params=pltpu.CompilerParams(vmem_limit_bytes=8 * 2**20),
        name="clip",
    )(parts, raw, bias)


def exchange(value, axes):
    return lax.all_to_all(value, axes, split_axis=0, concat_axis=0, tiled=True)


def local(tokens, weight, bias_term, cotangent):
    n_col = lax.axis_size("col")
    n_depth = lax.axis_size("depth")
    row_index = lax.axis_index("row")
    col = lax.axis_index("col")
    depth = lax.axis_index("depth")
    core = row_index % 2
    y = row_index // 2
    feat, ff = weight.shape
    share = cotangent.shape[0]
    block_ff = ff // n_depth
    tok = tokens.shape[0]
    half_ff = ff // 2

    def own_first(v):
        return jnp.where(core == 0, v, jnp.concatenate([v[tok:], v[:tok]], axis=0))

    got = [tokens] + [shift_row(tokens, k) for k in (1, 2, 3)]
    mine = jnp.stack([choose(got, (y - col - k) % 4) for k in REL])
    other = swap_core(mine)
    slice_x = jnp.concatenate([mine, other], axis=1).reshape(n_col * share, feat)

    up1, dn1 = shift_depth(mine, 1), shift_depth(mine, n_depth - 1)
    up2, dn2 = shift_depth(up1, 1), shift_depth(dn1, n_depth - 1)
    up3, dn3 = shift_depth(up2, 1), shift_depth(dn2, n_depth - 1)
    up4 = shift_depth(up3[: n_col // 2], 1)
    dn4 = shift_depth(dn3[n_col // 2 :], n_depth - 1)

    p1 = jnp.dot(slice_x, weight[:, :half_ff], preferred_element_type=F32).astype(BF)
    p1 = p1.reshape(n_col, share, half_ff)
    p2 = jnp.dot(slice_x, weight[:, half_ff:], preferred_element_type=F32).astype(BF)
    p2 = p2.reshape(n_col, share, half_ff)
    s1 = shift_col(p1[0], 1)
    s3 = shift_col(p2[0], 3)
    s5 = shift_col(jnp.concatenate([add_bf(s1, p1[1]), p2[1]], axis=1), 1)
    s6 = shift_col(jnp.concatenate([p1[2], add_bf(s3, p2[2])], axis=1), 3)
    o1 = p1[3].astype(F32) + s5[:, :half_ff].astype(F32) + s6[:, :half_ff].astype(F32)
    o2 = p2[3].astype(F32) + s6[:, half_ff:].astype(F32) + s5[:, half_ff:].astype(F32)
    preact = jnp.concatenate([o1, o2], axis=1) + bias_term
    activation, slope_term = gelu_parts(preact)
    grad_share = (own_first(cotangent).astype(F32) * slope_term).astype(BF)
    hidden_out = own_first(activation.astype(BF))

    later = after(grad_share, up3, dn3)
    b1 = shift_col(later, 1)
    b3 = shift_col(later, 3)
    b2 = shift_col(b1[:tok], 1)
    b4 = shift_col(b3[tok:], 3)
    columns = exchange(after(grad_share, up2, dn2).reshape(share, n_depth, block_ff).transpose(1, 0, 2), "depth")

    columns, b1, b3 = lax.optimization_barrier((columns, b1, b3))
    t_mine = stack_up([after(mine, columns), up1, up2, up3, up4, dn4, dn3, dn2, dn1])
    t_other = swap_core(t_mine)

    hz = n_depth // 2
    a1 = shift_col(columns, 1)
    d1 = shift_col(columns, 3)
    depth_arr = depth.astype(jnp.int32).reshape(1)
    at = {k: REL.index(k) for k in REL}
    grad_slice = jnp.concatenate([b2, b4, b3, b1, grad_share], axis=0)
    input_part = lax.dot_general(
        grad_slice, weight, (((1,), (1,)), ((), ())), preferred_element_type=F32
    ).reshape(n_col, 2, tok, feat)
    a1, d1, input_part = lax.optimization_barrier((a1, d1, input_part))
    a3 = shift_col(a1[:hz], 1)
    d3 = shift_col(d1[hz:], 3)
    acc = grad_step(
        t_mine,
        t_other,
        [(at[0], [columns]), (at[3], [a1]), (at[1], [d1])],
        None,
        depth_arr,
    )
    chip = input_part[:, 0] + swap_core(input_part[:, 1].astype(BF)).astype(F32)

    def rel_pos(k):
        d = (y + k - col) % 4
        return jnp.where(d == 2, 0, jnp.where(d == 1, 1, jnp.where(d == 3, 2, 3)))

    came = [shift_row(pick(chip, rel_pos(k)).astype(BF), k) for k in (1, 3, 2)]
    a3, d3, acc, came = lax.optimization_barrier((a3, d3, acc, came))
    first_col = (col == 0).astype(F32).reshape(1)
    raw, raw_bias, squares = grad_step(
        t_mine, t_other, [(at[2], [a3, d3])], acc, depth_arr, first_col
    )

    input_grad = pick(chip, rel_pos(0))
    for part in came:
        input_grad = input_grad + part.astype(F32)
    input_grad = input_grad.astype(BF)

    squares = jnp.sum(exchange(squares, ("row", "col")), axis=0, keepdims=True)
    squares = jnp.broadcast_to(squares, (n_depth,) + squares.shape[1:])
    weight_grad, bias_grad, grad_norm = clip(exchange(squares, "depth"), raw, raw_bias)
    return (input_grad, hidden_out, weight_grad, bias_grad, grad_norm[0])


def solution(mesh):
    in_specs = (P(("depth", "row"), "col"), P("col", "row"), P("row"), P(("depth", "col"), "row"))
    out_specs = (
        P(("depth", "row"), "col"),
        P(("depth", "col"), "row"),
        P("col", ("row", "depth")),
        P(("row", "depth")),
        P(),
    )
    return jax.shard_map(local, mesh=mesh, in_specs=in_specs, out_specs=out_specs, check_vma=False)
```

```python
import math

import jax
import jax.numpy as jnp
from jax import lax
from jax.experimental import pallas as pl
from jax.experimental.pallas import tpu as pltpu
from jax.sharding import PartitionSpec as P

D = 6144
FF = 24576

BF = jnp.bfloat16
F32 = jnp.float32
LANES = 128

gelu_scale = 0.7978845608
cubic_coef = 0.044715
norm_eps = 1e-06


def gelu_parts(preact):
    inside_term = gelu_scale * (preact + cubic_coef * preact * preact * preact)
    tanh_term = jnp.tanh(inside_term)
    activation = 0.5 * preact * (1.0 + tanh_term)
    slope_term = 0.5 * (1.0 + tanh_term) + 0.5 * preact * (
        1.0 - tanh_term * tanh_term
    ) * gelu_scale * (1.0 + 3.0 * cubic_coef * preact * preact)
    return (activation, slope_term)


def shift_row(value, k):
    n = lax.axis_size("row")
    return lax.ppermute(value, "row", [(i, (i + 2 * k) % n) for i in range(n)])


def swap_core(value):
    n = lax.axis_size("row")
    return lax.ppermute(value, "row", [(i, i ^ 1) for i in range(n)])


def shift_col(value, k):
    n = lax.axis_size("col")
    return lax.ppermute(value, "col", [(i, (i + k) % n) for i in range(n)])


def shift_depth(value, k):
    n = lax.axis_size("depth")
    return lax.ppermute(value, "depth", [(i, (i + k) % n) for i in range(n)])


def after(value, *others):
    return lax.optimization_barrier((value, *others))[0]


def add_bf(a, b):
    return (a.astype(F32) + b.astype(F32)).astype(BF)


def pick(stack, index):
    return lax.dynamic_index_in_dim(stack, index, 0, keepdims=False)


def choose(options, index):
    res = options[-1]
    for i in range(len(options) - 1):
        res = jnp.where(index == i, options[i], res)
    return res


def stack_kernel(*refs):
    *srcs, dst, held, sems = refs
    n_share = held.shape[1]
    ins, outs, low = [], [], 0
    for i, src in enumerate(srcs):
        size = src.shape[0]
        slot = held.at[low // n_share, low % n_share : low % n_share + size]
        out = dst.at[low // n_share, low % n_share : low % n_share + size]
        ins.append(pltpu.make_async_copy(src, slot, sems.at[0, i]))
        outs.append(pltpu.make_async_copy(slot, out, sems.at[1, i]))
        low += size
    for c in ins:
        c.start()
    for c, d in zip(ins, outs):
        c.wait()
        d.start()
    for d in outs:
        d.wait()


def stack_up(pieces):
    one = pieces[0]
    shape = (sum(p.shape[0] for p in pieces) // one.shape[0],) + one.shape
    return pl.pallas_call(
        stack_kernel,
        in_specs=[pl.BlockSpec(memory_space=pl.ANY)] * len(pieces),
        out_specs=pl.BlockSpec(memory_space=pl.ANY),
        out_shape=jax.ShapeDtypeStruct(shape, one.dtype),
        scratch_shapes=[
            pltpu.VMEM(shape, one.dtype),
            pltpu.SemaphoreType.DMA((2, len(pieces))),
        ],
        compiler_params=pltpu.CompilerParams(vmem_limit_bytes=56 * 2**20),
        cost_estimate=pl.CostEstimate(
            flops=0, bytes_accessed=4 * math.prod(shape), transcendentals=0
        ),
        name="stack_up",
    )(*pieces)


REL = (2, 1, 3, 0)


def grad_step(t_mine, t_other, pieces, acc, depth, first_col=None):
    n_depth, n_share, rows, feat = t_mine.shape
    block_ff = pieces[0][1][0].shape[-1]
    width = 1536
    kdim = n_depth * rows
    n_p = len(pieces)
    counts = [len(p[1]) for p in pieces]
    flat = [b for p in pieces for b in p[1]]
    final = first_col is not None
    have = acc is not None

    def body(*refs):
        refs = list(refs)
        depth_ref = refs.pop(0)
        first_ref = refs.pop(0) if final else None
        t_refs = [(refs.pop(0), refs.pop(0)) for _ in range(n_p)]
        g_refs = [refs.pop(0) for _ in flat]
        acc_ref, bias_in = (refs.pop(0), refs.pop(0)) if have else (None, None)
        out_ref, bias_out = refs.pop(0), refs.pop(0)
        sq_out = refs.pop(0) if final else None
        stage, gt = refs.pop(0), refs.pop(0)
        total = refs.pop(0) if final else None
        step = pl.program_id(0)

        @pl.when(step == 0)
        def _():
            me = depth_ref[0]
            bias = jnp.zeros((1, block_ff), F32)
            if have:
                bias = bias_in[...]
            at = 0
            for i in range(n_p):
                low = 0
                for _ in range(counts[i]):
                    g = g_refs[at]
                    at += 1
                    size = g.shape[0]
                    stage[low : low + size] = g[...]
                    low += size
                whole = stage[...].reshape(n_depth * 2 * rows, block_ff)
                bias = bias + jnp.sum(whole.astype(F32), axis=0, keepdims=True)
                for half in range(2):
                    parts = []
                    for d in range(n_depth):
                        z = lax.rem(me + n_depth - d, n_depth)
                        parts.append(stage[z, half * rows : (half + 1) * rows, :])
                    gt[2 * i + half] = jnp.concatenate(parts, axis=0).T
            bias_out[...] = bias

        res = acc_ref[...] if have else None
        for i in range(n_p):
            for half in range(2):
                t = t_refs[i][half][...].reshape(kdim, width)
                one = jnp.dot(gt[2 * i + half], t, preferred_element_type=F32)
                res = one if res is None else res + one
        out_ref[...] = res
        if final:
            here = jnp.sum(res * res, keepdims=True)

            @pl.when(step == 0)
            def _():
                b = bias_out[...]
                total[...] = here + first_ref[0] * jnp.sum(b * b, keepdims=True)

            @pl.when(step > 0)
            def _():
                total[...] += here

            sq_out[...] = jnp.broadcast_to(total[...].reshape(1, 1, 1), sq_out.shape)

    smem = pl.BlockSpec(memory_space=pltpu.SMEM)

    def whole_spec(shape):
        return pl.BlockSpec(shape, lambda j: (0,) * len(shape))

    def t_spec(pos):
        return pl.BlockSpec((n_depth, 1, rows, width), lambda j: (0, pos, 0, j))

    acc_spec = pl.BlockSpec((block_ff, width), lambda j: (0, j))
    bias_spec = whole_spec((1, block_ff))
    ins = [depth] + ([first_col] if final else [])
    specs = [smem] * len(ins)
    for pos, _ in pieces:
        ins += [t_mine, t_other]
        specs += [t_spec(pos)] * 2
    ins += flat
    specs += [whole_spec(b.shape) for b in flat]
    if have:
        ins += list(acc)
        specs += [acc_spec, bias_spec]
    out_shape = [
        jax.ShapeDtypeStruct((block_ff, feat), F32),
        jax.ShapeDtypeStruct((1, block_ff), F32),
    ]
    out_specs = [acc_spec, bias_spec]
    scratch = [
        pltpu.VMEM((n_depth, 2 * rows, block_ff), BF),
        pltpu.VMEM((2 * n_p, block_ff, kdim), BF),
    ]
    if final:
        n_sq = lax.axis_size(("row", "col"))
        out_shape.append(jax.ShapeDtypeStruct((n_sq, 1, LANES), F32))
        out_specs.append(whole_spec((n_sq, 1, LANES)))
        scratch.append(pltpu.VMEM((1, 1), F32))
    return pl.pallas_call(
        body,
        grid=(feat // width,),
        in_specs=specs,
        out_specs=out_specs,
        out_shape=out_shape,
        scratch_shapes=scratch,
        compiler_params=pltpu.CompilerParams(vmem_limit_bytes=24 * 2**20),
        cost_estimate=pl.CostEstimate(
            flops=n_p * 4 * kdim * block_ff * feat,
            bytes_accessed=n_p * 4 * kdim * feat + 8 * block_ff * feat,
            transcendentals=0,
        ),
        name="grad_step",
    )(*ins)


def clip(parts, raw, bias):
    block_ff, feat = raw.shape
    width = 768

    def body(p, r, b, o, ob, on):
        total = jnp.sum(p[...], axis=0)[:, :1]
        norm = jnp.sqrt(total + norm_eps)
        factor = jnp.minimum(1.0, math.sqrt(D * FF) / norm)
        o[...] = r[...].T * factor
        ob[...] = (b[...] * factor).reshape(block_ff)
        on[0] = norm[0, 0]

    def whole_spec(shape):
        return pl.BlockSpec(shape, lambda j: (0,) * len(shape))

    return pl.pallas_call(
        body,
        grid=(feat // width,),
        in_specs=[
            whole_spec(parts.shape),
            pl.BlockSpec((block_ff, width), lambda j: (0, j)),
            whole_spec((1, block_ff)),
        ],
        out_specs=[
            pl.BlockSpec((width, block_ff), lambda j: (j, 0)),
            whole_spec((block_ff,)),
            pl.BlockSpec(memory_space=pltpu.SMEM),
        ],
        out_shape=[
            jax.ShapeDtypeStruct((feat, block_ff), F32),
            jax.ShapeDtypeStruct((block_ff,), F32),
            jax.ShapeDtypeStruct((1,), F32),
        ],
        compiler_params=pltpu.CompilerParams(vmem_limit_bytes=8 * 2**20),
        name="clip",
    )(parts, raw, bias)


def exchange(value, axes):
    return lax.all_to_all(value, axes, split_axis=0, concat_axis=0, tiled=True)


def local(tokens, weight, bias_term, cotangent):
    n_col = lax.axis_size("col")
    n_depth = lax.axis_size("depth")
    row_index = lax.axis_index("row")
    col = lax.axis_index("col")
    depth = lax.axis_index("depth")
    core = row_index % 2
    y = row_index // 2
    feat, ff = weight.shape
    share = cotangent.shape[0]
    block_ff = ff // n_depth
    tok = tokens.shape[0]
    half_ff = ff // 2

    def own_first(v):
        return jnp.where(core == 0, v, jnp.concatenate([v[tok:], v[:tok]], axis=0))

    far = shift_row(tokens, 2)
    got = [tokens, shift_row(tokens, 1), far, shift_row(tokens, 3)]
    mine = jnp.stack([choose(got, (y - col - k) % 4) for k in REL])
    other = swap_core(mine)
    slice_x = jnp.concatenate([mine, other], axis=1).reshape(n_col * share, feat)

    up1, dn1 = shift_depth(mine, 1), shift_depth(mine, n_depth - 1)
    up2, dn2 = shift_depth(up1, 1), shift_depth(dn1, n_depth - 1)
    up3, dn3 = shift_depth(up2, 1), shift_depth(dn2, n_depth - 1)
    up4 = shift_depth(up3[: n_col // 2], 1)
    dn4 = shift_depth(dn3[n_col // 2 :], n_depth - 1)

    p1 = jnp.dot(slice_x, weight[:, :half_ff], preferred_element_type=F32).astype(BF)
    p1 = p1.reshape(n_col, share, half_ff)
    p2 = jnp.dot(slice_x, weight[:, half_ff:], preferred_element_type=F32).astype(BF)
    p2 = p2.reshape(n_col, share, half_ff)
    s1 = shift_col(p1[0], 1)
    s3 = shift_col(p2[0], 3)
    s5 = shift_col(jnp.concatenate([add_bf(s1, p1[1]), p2[1]], axis=1), 1)
    s6 = shift_col(jnp.concatenate([p1[2], add_bf(s3, p2[2])], axis=1), 3)
    o1 = p1[3].astype(F32) + s5[:, :half_ff].astype(F32) + s6[:, :half_ff].astype(F32)
    o2 = p2[3].astype(F32) + s6[:, half_ff:].astype(F32) + s5[:, half_ff:].astype(F32)
    preact = jnp.concatenate([o1, o2], axis=1) + bias_term
    activation, slope_term = gelu_parts(preact)
    grad_share = (own_first(cotangent).astype(F32) * slope_term).astype(BF)
    hidden_out = own_first(activation.astype(BF))

    later = after(grad_share, up3, dn3)
    b1 = shift_col(later, 1)
    b3 = shift_col(later, 3)
    b2 = shift_col(b1[:tok], 1)
    b4 = shift_col(b3[tok:], 3)
    columns = exchange(grad_share.reshape(share, n_depth, block_ff).transpose(1, 0, 2), "depth")

    columns, b1, b3 = lax.optimization_barrier((columns, b1, b3))
    t_mine = stack_up([after(mine, columns), up1, up2, up3, up4, dn4, dn3, dn2, dn1])
    t_other = swap_core(t_mine)

    hz = n_depth // 2
    a1 = shift_col(columns, 1)
    d1 = shift_col(columns, 3)
    depth_arr = depth.astype(jnp.int32).reshape(1)
    at = {k: REL.index(k) for k in REL}
    grad_slice = jnp.concatenate([b2, b4, b3, b1, grad_share], axis=0)
    input_part = lax.dot_general(
        grad_slice, weight, (((1,), (1,)), ((), ())), preferred_element_type=F32
    ).reshape(n_col, 2, tok, feat)
    a1, d1, input_part = lax.optimization_barrier((a1, d1, input_part))
    a3 = shift_col(a1[:hz], 1)
    d3 = shift_col(d1[hz:], 3)
    acc = grad_step(
        t_mine,
        t_other,
        [(at[0], [columns]), (at[3], [a1]), (at[1], [d1])],
        None,
        depth_arr,
    )
    chip = input_part[:, 0] + swap_core(input_part[:, 1].astype(BF)).astype(F32)

    def rel_pos(k):
        d = (y + k - col) % 4
        return jnp.where(d == 2, 0, jnp.where(d == 1, 1, jnp.where(d == 3, 2, 3)))

    came = [shift_row(pick(chip, rel_pos(k)).astype(BF), k) for k in (2, 1, 3)]
    a3, d3, acc, came = lax.optimization_barrier((a3, d3, acc, came))
    first_col = (col == 0).astype(F32).reshape(1)
    raw, raw_bias, squares = grad_step(
        t_mine, t_other, [(at[2], [a3, d3])], acc, depth_arr, first_col
    )

    input_grad = pick(chip, rel_pos(0))
    for part in came:
        input_grad = input_grad + part.astype(F32)
    input_grad = input_grad.astype(BF)

    squares = jnp.sum(exchange(squares, ("row", "col")), axis=0, keepdims=True)
    squares = jnp.broadcast_to(squares, (n_depth,) + squares.shape[1:])
    weight_grad, bias_grad, grad_norm = clip(exchange(squares, "depth"), raw, raw_bias)
    return (input_grad, hidden_out, weight_grad, bias_grad, grad_norm[0])


def solution(mesh):
    in_specs = (P(("depth", "row"), "col"), P("col", "row"), P("row"), P(("depth", "col"), "row"))
    out_specs = (
        P(("depth", "row"), "col"),
        P(("depth", "col"), "row"),
        P("col", ("row", "depth")),
        P(("row", "depth")),
        P(),
    )
    return jax.shard_map(local, mesh=mesh, in_specs=in_specs, out_specs=out_specs, check_vma=False)
```
